32 devices in a mesh: dp: 16 (over z, y, core), shard: 2 (over x).
Axes of the slice: x: 2, y: 2, z: 4, core: 2. Of those that a mesh axis runs over, the one named last changes fastest.
Arguments:
- resid_in: bfloat16 [2048, 8192], P('dp', 'shard'), may hold values from -6 to 6
- hidden: bfloat16 [2048, 28672], P('shard', 'dp'), may hold values from -6 to 6
- w_down: bfloat16 [28672, 8192], P('dp', 'shard'), may hold values from -0.03125 to 0.03125
- frozen: bfloat16 [2048, 8192], P(('dp', 'shard')), may hold values from -6 to 6
- steer: bfloat16 [8192], P('shard'), may hold values from -6 to 6
- forget_flags: int32 [8], replicated, may hold values from 0 to 1, as said below
Outputs:
- updated: bfloat16 [2048, 8192], P('dp', 'shard')
- grad_down: float32 [28672, 8192], P('dp', 'shard')
The draws below stay inside these ranges and needn't reach their ends.
Inputs may be any that keep to these rules, and one draw needn't show every extreme that they name: `forget_flags`: exactly half of the 8 sequences are forget sequences.
All inputs are finite; a program needn't handle non-finite values.
Results may differ from the reference program's by a relative error of at most 0.0019.
Values may be sent and summed in bfloat16 or wider, within the bound.
No kernel may reach another device: no remote copies, remote signals or barrier semaphores. Data moves between devices by JAX's collectives and lax.ppermute only.
A program may use at most 192 MiB of HBM per device.

```python
import math
import jax
import jax.numpy as jnp
from jax import lax

D = 8192
FF = 28672
SEQ_LEN = 256
TOKENS = 2048
SEQS = 8


def draw_forget_flags(key, part):
    order = jax.random.permutation(key, SEQS)
    return (order < SEQS // 2).astype(jnp.int32)


def spiked(result, key, source, target, blocks, factor):
    owner, partner = [(jnp.arange(result.shape[axis_at]) // (result.shape[axis_at] // blocks)).reshape([-1 if axis == axis_at else 1 for axis in range(result.ndim)]) for axis_at in (source, target)]
    chosen = jax.random.permutation(key, blocks)[partner]
    strong = (owner == chosen) | (owner == (partner + blocks // 2) % blocks)
    return jnp.where(strong, factor * result, result)


def steps_of(own_key, shape, pieces, low, high):
    factor_of, own = 1.0, jax.random.fold_in(own_key, 6)
    for axis_at, blocks in pieces:
        heights = jnp.exp(jax.random.uniform(jax.random.fold_in(own, axis_at), (blocks,), jnp.float32, low / len(pieces), high / len(pieces)))
        factor_of = factor_of * jnp.repeat(heights, shape[axis_at] // blocks).reshape([-1 if axis == axis_at else 1 for axis in range(len(shape))])
    return factor_of


def bell_draw(key, dims, spread, limit, cuts=(), held_as=jnp.bfloat16):
    entries = jax.random.normal(key, dims, jnp.float32) * spread
    if len(cuts) > 0:
        entries = steps_of(key, dims, cuts, -0.22, 0.18) * entries
    return jnp.clip(entries, min=-limit, max=limit).astype(held_as)


def heavy_noise(stream_key, shape, deviation, reach, shards, heavy, kind=jnp.bfloat16):
    entries = deviation * jax.random.normal(stream_key, shape, jnp.float32)
    if shards:
        entries = entries * steps_of(stream_key, shape, shards, -0.22, 0.18)
    return jnp.clip(spiked(entries, jax.random.fold_in(stream_key, 3), *heavy), -reach, reach).astype(kind)


def setup_inputs(seed: int = 0) -> dict:
    key_list = jax.random.split(jax.random.key(seed), 7)
    resid_in = bell_draw(key_list[0], (TOKENS, D), 1.0, 6.0, ((0, 16), (1, 2)))
    hidden = heavy_noise(key_list[1], (TOKENS, FF), 1.0, 6.0, ((0, 2), (1, 16)), (1, 0, 16, 2.0))
    w_down = bell_draw(key_list[2], (FF, D), FF ** -0.5, 0.03125, ((0, 16), (1, 2)))
    frozen = bell_draw(key_list[3], (TOKENS, D), 1.0, 6.0, ((0, 32),))
    steer = bell_draw(key_list[4], (D,), 1.0, 6.0, ((0, 2),))
    forget_flags = draw_forget_flags(jax.random.fold_in(key_list[6], 71), 0)
    return {"resid_in": resid_in, "hidden": hidden, "w_down": w_down, "frozen": frozen, "steer": steer, "forget_flags": forget_flags}


retain_weight = 2.0

def reference(resid_in, hidden, w_down, frozen, steer, forget_flags):
    mlp_out = jnp.dot(hidden, w_down, preferred_element_type=jnp.float32)
    residual = resid_in.astype(jnp.float32) + mlp_out
    updated = residual.astype(jnp.bfloat16)
    seq_ids = (jnp.arange(TOKENS, dtype=jnp.int32) // SEQ_LEN).astype(jnp.int32)
    is_forget = forget_flags[seq_ids] > 0
    target = jnp.where(is_forget[:, None], steer.astype(jnp.float32)[None, :], frozen.astype(jnp.float32))
    loss_weight = jnp.where(is_forget, 1.0, retain_weight).astype(jnp.float32)
    slopes = (loss_weight[:, None] * (residual - target) * (1.0 / math.sqrt(TOKENS))).astype(jnp.bfloat16)
    grad_down = lax.dot_general(hidden, slopes, (((0,), (0,)), ((), ())), preferred_element_type=jnp.float32)
    return (updated, grad_down)
```

```python
import math

import jax
import jax.numpy as jnp
from jax import lax
from jax.experimental import pallas as pl
from jax.experimental.pallas import tpu as pltpu
from jax.sharding import PartitionSpec as P

SEQ_LEN = 256
RETAIN_WEIGHT = 2.0
F32, BF16, WIRE = jnp.float32, jnp.bfloat16, jnp.float16
VMEM_LIMIT = 56 * 1024 * 1024


def bits_of(count):
    return count.bit_length() - 1


def flip(array, axis, mask):
    return lax.ppermute(array, axis, [(i, i ^ mask) for i in range(lax.axis_size(axis))])


def slot_of(chip, nb):
    slot = 0
    for b in range(nb):
        slot = slot * 2 + ((chip >> b) & 1)
    return slot


def project(place, groups, w_down, nb):
    per, _, rows, units = groups[0].shape
    chips, feats = 2**nb, w_down.shape[1]
    block = min(1024, feats)

    def kernel(place_ref, *refs):
        group_refs, (w_ref, theirs_ref, mine_ref, rows_ref) = refs[: len(groups)], refs[len(groups) :]

        @pl.when(pl.program_id(0) == 0)
        def _():
            core, chip, shard = place_ref[0], place_ref[1], place_ref[2]
            for d, group_ref in enumerate(group_refs):
                for t in range(per):
                    slot = slot_of(chip ^ ((shard ^ d) * per + t), nb)
                    for parity in range(2):
                        rows_ref[core ^ parity, slot] = group_ref[t, parity]

        for parity, out_ref in ((1, theirs_ref), (0, mine_ref)):
            lhs = rows_ref[parity].reshape(chips * rows, units)
            out_ref[...] = jnp.dot(lhs, w_ref[...], preferred_element_type=F32)

    whole = [pl.BlockSpec(g.shape, lambda i, _: (0, 0, 0, 0)) for g in groups]
    column = pl.BlockSpec((chips * rows, block), lambda i, _: (0, i))
    partial = jax.ShapeDtypeStruct((chips * rows, feats), F32)
    return pl.pallas_call(
        kernel,
        grid_spec=pltpu.PrefetchScalarGridSpec(
            num_scalar_prefetch=1,
            grid=(feats // block,),
            in_specs=whole + [pl.BlockSpec((units, block), lambda i, _: (0, i))],
            out_specs=[column, column, pl.BlockSpec((2, chips, rows, units), lambda i, _: (0, 0, 0, 0))],
        ),
        out_shape=[partial, partial, jax.ShapeDtypeStruct((2, chips, rows, units), BF16)],
        compiler_params=pltpu.CompilerParams(vmem_limit_bytes=VMEM_LIMIT),
        cost_estimate=pl.CostEstimate(
            flops=4 * chips * rows * units * feats,
            bytes_accessed=2 * units * feats + 8 * chips * rows * feats + 8 * chips * rows * units,
            transcendentals=0,
        ),
    )(place, *groups, w_down)


def gradient(chunks, slopes, grad, start, feats):
    units, width = chunks[0].shape[3], slopes[0].shape[2]
    block = min(512, width)
    first = start // block

    def kernel(*refs):
        chunk_refs, slope_refs = refs[: len(chunks)], refs[len(chunks) : len(chunks) + 2]
        total, row = None, 0
        for ref in chunk_refs:
            _, chips, rows, _ = ref.shape
            for parity in range(2):
                term = lax.dot_general(
                    ref[parity].reshape(chips * rows, units),
                    slope_refs[parity][:, row : row + rows].reshape(chips * rows, block),
                    (((0,), (0,)), ((), ())),
                    preferred_element_type=F32,
                )
                total = term if total is None else total + term
            row += rows
        refs[-1][...] = total

    tokens = 2 * slopes[0].shape[0] * slopes[0].shape[1]
    in_specs = [pl.BlockSpec(c.shape, lambda i: (0, 0, 0, 0)) for c in chunks]
    in_specs += [pl.BlockSpec(s.shape[:2] + (block,), lambda i: (0, 0, i)) for s in slopes]
    args, alias = [*chunks, *slopes], {}
    if grad is not None:
        alias = {len(args): 0}
        args.append(grad)
        in_specs.append(pl.BlockSpec(memory_space=pl.ANY))
    return pl.pallas_call(
        kernel,
        grid=(width // block,),
        in_specs=in_specs,
        out_specs=pl.BlockSpec((units, block), lambda i: (0, first + i)),
        out_shape=jax.ShapeDtypeStruct((units, feats), F32),
        input_output_aliases=alias,
        compiler_params=pltpu.CompilerParams(vmem_limit_bytes=VMEM_LIMIT),
        cost_estimate=pl.CostEstimate(
            flops=2 * tokens * units * width,
            bytes_accessed=2 * tokens * (units + width) + 4 * units * width,
            transcendentals=0,
        ),
    )(*args)


def reduce_chips(total, order, nb):
    total = total.reshape((2,) * nb + total.shape[1:])
    left = list(range(nb))
    for b in order:
        at = left.index(b)
        sent = lax.index_in_dim(total, 1, at, keepdims=False).astype(WIRE)
        kept = lax.index_in_dim(total, 0, at, keepdims=False)
        total = kept.astype(F32) + flip(sent, "dp", 2 << b).astype(F32)
        left.remove(b)
    return total


def gather_chips(block, order, nb):
    have = []
    for b in order:
        have = sorted([*have, b])
        block = jnp.stack([block, flip(block, "dp", 2 << b)], axis=have.index(b))
    return block.reshape((2**nb,) + block.shape[nb:])


def per_device(resid_in, hidden, w_down, frozen, steer, forget_flags):
    n_dp, n_shard = lax.axis_size("dp"), lax.axis_size("shard")
    chips = n_dp // 2
    nb = bits_of(chips)
    tok_rows, feats = resid_in.shape
    units = hidden.shape[1]
    dp, shard = lax.axis_index("dp"), lax.axis_index("shard")
    core, chip = dp % 2, dp // 2
    place = jnp.stack([core, chip, shard]).astype(jnp.int32)
    spans = [tok_rows // 4] * 4
    quarters = 4

    own = hidden.reshape(chips // n_shard, 2, tok_rows, units)
    groups, row = [], 0
    for rows in spans:
        part = lax.slice_in_dim(own, row, row + rows, axis=2)
        groups.append([part] + [flip(part, "shard", d) for d in range(1, n_shard)])
        row += rows

    target_rows = lax.all_to_all(frozen, "shard", split_axis=1, concat_axis=0, tiled=True)
    seq = (dp * tok_rows + jnp.arange(tok_rows, dtype=jnp.int32)) // SEQ_LEN
    match = seq[:, None] == jnp.arange(forget_flags.shape[0], dtype=jnp.int32)[None, :]
    is_forget = jnp.sum(jnp.where(match, forget_flags[None, :], 0), axis=1, keepdims=True) > 0
    scale = jnp.where(is_forget, 1.0, RETAIN_WEIGHT).astype(F32) * (1.0 / math.sqrt(tok_rows * n_dp))
    target = jnp.where(is_forget, steer.astype(F32)[None, :], target_rows.astype(F32))

    updated, slopes, chunks, row = [], [], [], 0
    for k, rows in enumerate(spans):
        theirs, mine, chunk = project(place, groups[k], w_down, nb)
        chunks.append(chunk)
        total = (mine + flip(theirs, "dp", 1)).reshape(chips, rows, feats)
        order = list(range(nb))
        mlp_out = reduce_chips(total, order, nb)
        here = slice(row, row + rows)
        residual = resid_in[here].astype(F32) + mlp_out
        updated.append(residual.astype(BF16))
        slopes.append((scale[here] * (residual - target[here])).astype(BF16))
        row += rows
    updated = jnp.concatenate(updated)
    slopes = jnp.concatenate(slopes)

    grad, width = None, feats // quarters
    for q in range(quarters):
        order = list(reversed(range(nb)))
        mine = gather_chips(slopes[:, q * width : (q + 1) * width], order, nb)
        theirs = flip(mine, "dp", 1)
        grad = gradient(chunks, [mine, theirs], grad, q * width, feats)
    return updated, grad


def solution(mesh):
    in_specs = (
        P("dp", "shard"),
        P("shard", "dp"),
        P("dp", "shard"),
        P(("dp", "shard"), None),
        P("shard"),
        P(),
    )
    out_specs = (P("dp", "shard"), P("dp", "shard"))
    return jax.shard_map(
        per_device, mesh=mesh, in_specs=in_specs, out_specs=out_specs, check_vma=False
    )
```

```python
import math

import jax
import jax.numpy as jnp
from jax import lax
from jax.experimental import pallas as pl
from jax.experimental.pallas import tpu as pltpu
from jax.sharding import PartitionSpec as P

SEQ_LEN = 256
RETAIN_WEIGHT = 2.0
F32, BF16, WIRE = jnp.float32, jnp.bfloat16, jnp.float16
VMEM_LIMIT = 56 * 1024 * 1024


def bits_of(count):
    return count.bit_length() - 1


def flip(array, axis, mask):
    return lax.ppermute(array, axis, [(i, i ^ mask) for i in range(lax.axis_size(axis))])


def slot_of(chip, nb):
    slot = 0
    for b in range(nb):
        slot = slot * 2 + ((chip >> b) & 1)
    return slot


def project(place, groups, rows, at, w_down, start, width, held, before):
    arrays = [g for g, _ in groups]
    units = w_down.shape[0]
    chips, tok_rows = (held.shape[1:3]) if held is not None else (arrays[0].shape[0] * len(arrays), arrays[0].shape[2])
    nb = bits_of(chips)
    block = min(1024, width)
    first = start // block

    def kernel(place_ref, *refs):
        group_refs, w_ref = refs[: len(arrays)], refs[len(arrays)]
        if arrays:
            theirs_ref, mine_ref, rows_ref = refs[-3:]

            @pl.when(pl.program_id(0) == 0)
            def _():
                for d, (ref, (_, from_row)) in enumerate(zip(group_refs, groups)):
                    per = ref.shape[0]
                    for t in range(per):
                        slot = slot_of(place_ref[1] ^ ((place_ref[2] ^ d) * per + t), nb)
                        for parity in range(2):
                            rows_ref[place_ref[0] ^ parity, slot] = ref[t, parity, from_row : from_row + rows]

        else:
            (theirs_ref, mine_ref), rows_ref = refs[-2:], refs[1]
        for parity, out_ref in ((1, theirs_ref), (0, mine_ref)):
            lhs = rows_ref[parity].reshape(chips * rows, units)
            out_ref[...] = jnp.dot(lhs, w_ref[...], preferred_element_type=F32)

    chunk = pl.BlockSpec((2, chips, rows, units), lambda i, _: (0, 0, at // rows, 0))
    column = pl.BlockSpec((chips * rows, block), lambda i, _: (0, i))
    partial = jax.ShapeDtypeStruct((chips * rows, width), F32)
    out_specs, out_shape, alias = [column, column], [partial, partial], {}
    args = [*arrays, w_down]
    in_specs = [pl.BlockSpec(g.shape, lambda i, _: (0, 0, 0, 0)) for g in arrays]
    in_specs.append(pl.BlockSpec((units, block), lambda i, _: (0, first + i)))
    if arrays:
        out_specs.append(chunk)
        out_shape.append(jax.ShapeDtypeStruct((2, chips, tok_rows, units), BF16))
    if held is not None:
        if arrays:
            alias = {len(args) + 1: 2}
        args.append(held)
        in_specs.append(pl.BlockSpec(memory_space=pl.ANY) if arrays else chunk)
    args += before
    in_specs += [pl.BlockSpec(memory_space=pl.ANY)] * len(before)
    return pl.pallas_call(
        kernel,
        grid_spec=pltpu.PrefetchScalarGridSpec(
            num_scalar_prefetch=1, grid=(width // block,), in_specs=in_specs, out_specs=out_specs
        ),
        out_shape=out_shape,
        input_output_aliases=alias,
        compiler_params=pltpu.CompilerParams(vmem_limit_bytes=VMEM_LIMIT),
        cost_estimate=pl.CostEstimate(
            flops=4 * chips * rows * units * width,
            bytes_accessed=2 * units * width + 8 * chips * rows * (width + units),
            transcendentals=0,
        ),
    )(place, *args)


def gradient(place, rows, firsts, slopes):
    _, chips, tok_rows, units = rows.shape
    counts, feats = [f.shape[1] for f in firsts], firsts[0].shape[2]
    count = sum(counts)
    width = slopes[0][0].shape[2]
    nb = bits_of(chips)
    block = min(512, width)
    each = width // block

    def kernel(place_ref, rows_ref, *refs):
        first_refs, refs = refs[: len(firsts)], refs[len(firsts) :]
        out_ref, all_ref = refs[-2:]
        for parity in range(2):
            for owner in range(chips):
                slot, row = slot_of(place_ref[1] ^ owner, nb), 0
                for n, first_ref in zip(counts, first_refs):
                    all_ref[parity, slot, row : row + n] = first_ref[2 * owner + (place_ref[0] ^ parity)]
                    row += n
        for q in range(len(slopes)):

            @pl.when(pl.program_id(0) // each == q)
            def _():
                for parity in range(2):
                    all_ref[parity, :, count:] = refs[2 * q + parity][...]

        total = None
        for parity in range(2):
            term = lax.dot_general(
                rows_ref[parity].reshape(chips * tok_rows, units),
                all_ref[parity].reshape(chips * tok_rows, block),
                (((0,), (0,)), ((), ())),
                preferred_element_type=F32,
            )
            total = term if total is None else total + term
        out_ref[...] = total

    in_specs = [
        pl.BlockSpec(rows.shape, lambda i, _: (0, 0, 0, 0), pipeline_mode=pl.Buffered(1)),
        *[pl.BlockSpec((2 * chips, n, block), lambda i, _: (0, 0, i)) for n in counts],
    ]
    for q in range(len(slopes)):
        in_specs += [
            pl.BlockSpec(
                (chips, tok_rows - count, block), lambda i, _, q=q: (0, 0, jnp.clip(i - q * each, 0, each - 1))
            )
        ] * 2
    return pl.pallas_call(
        kernel,
        grid_spec=pltpu.PrefetchScalarGridSpec(
            num_scalar_prefetch=1,
            grid=(feats // block,),
            in_specs=in_specs,
            out_specs=pl.BlockSpec((units, block), lambda i, _: (0, i)),
            scratch_shapes=[pltpu.VMEM((2, chips, tok_rows, block), BF16)],
        ),
        out_shape=jax.ShapeDtypeStruct((units, feats), F32),
        compiler_params=pltpu.CompilerParams(vmem_limit_bytes=VMEM_LIMIT),
        cost_estimate=pl.CostEstimate(
            flops=4 * chips * tok_rows * units * feats,
            bytes_accessed=4 * chips * tok_rows * (units + feats) + 4 * units * feats,
            transcendentals=0,
        ),
    )(place, rows, *firsts, *[s for pair in slopes for s in pair])


def cut(total, left, b):
    at = left.index(b)
    sent = lax.index_in_dim(total, 1, at, keepdims=False).astype(WIRE)
    return lax.index_in_dim(total, 0, at, keepdims=False), flip(sent, "dp", 2 << b)


def nothing(array):
    return array[(0,) * array.ndim] * 0


def gather_chips(block, order):
    have = []
    for b in order:
        have = sorted([*have, b])
        block = jnp.stack([block, flip(block, "dp", 2 << b)], axis=have.index(b))
    return block.reshape((2 ** len(order),) + block.shape[len(order) :])


def pass_pair(array):
    pieces = jnp.split(array.astype(WIRE), 4, axis=0)
    return jnp.concatenate([flip(p, "dp", 1) for p in pieces]).astype(F32)


def per_device(resid_in, hidden, w_down, frozen, steer, forget_flags):
    n_dp, n_shard = lax.axis_size("dp"), lax.axis_size("shard")
    chips = n_dp // 2
    nb = bits_of(chips)
    tok_rows, feats = resid_in.shape
    units = hidden.shape[1]
    dp, shard = lax.axis_index("dp"), lax.axis_index("shard")
    core, chip = dp % 2, dp // 2
    place = jnp.stack([core, chip, shard]).astype(jnp.int32)
    up = list(range(nb))
    orders = [up, [*up[1:2], *up[:1], *up[2:]]]
    half = feats // 2
    unit = tok_rows // 8
    spans = [unit * n for n in (3, 3, 2)]
    starts = [sum(spans[:k]) for k in range(len(spans))]
    sends = [(0, spans[0]), (spans[0], tok_rows)]

    def pick(stack, at):
        return lax.dynamic_index_in_dim(stack, at, 0, keepdims=False)

    own = hidden.reshape(chips // n_shard, 2, tok_rows, units)
    far = [
        [flip(lax.slice_in_dim(own, at, end, axis=2), "shard", d) for d in range(1, n_shard)] for at, end in sends
    ]
    found = []
    for d in range(n_shard):
        part = lax.dynamic_slice_in_dim(frozen, (shard ^ d) * feats, feats, axis=1)
        if d:
            part = flip(part + nothing(far[0][0]), "shard", d)
        found.append(part)
    found = jnp.stack(found)
    target_rows = jnp.concatenate([pick(found, shard ^ e) for e in range(n_shard)])
    seq = (dp * tok_rows + jnp.arange(tok_rows, dtype=jnp.int32)) // SEQ_LEN
    match = seq[:, None] == jnp.arange(forget_flags.shape[0], dtype=jnp.int32)[None, :]
    is_forget = jnp.sum(jnp.where(match, forget_flags[None, :], 0), axis=1, keepdims=True) > 0
    scale = jnp.where(is_forget, 1.0, RETAIN_WEIGHT).astype(F32) * (1.0 / math.sqrt(tok_rows * n_dp))
    target = jnp.where(is_forget, steer.astype(F32)[None, :], target_rows.astype(F32))

    held, firsts, updated, sloped, sums = None, [], [], [], {}

    def multiply(k, s, before):
        nonlocal held
        piece = min(k, 1)
        source = [] if s else [(own, starts[k])] + [(f, starts[k] - sends[piece][0]) for f in far[piece]]
        theirs, mine, *out = project(place, source, spans[k], starts[k], w_down, s * half, half, held, before)
        held = out[0] if out else held
        sums[k, s] = mine, pass_pair(theirs), orders[s]
        return nothing(theirs)

    def advance(k, zero):
        kept_all, changed, slopes = [], [], []
        for s in range(len(orders)):
            kept, came, order = sums[k, s]
            total = kept + came.astype(F32) + zero
            if len(order) == nb:
                total = total.reshape((2,) * nb + (spans[k], half))
            if order:
                sums[k, s] = *cut(total, sorted(order), order[0]), order[1:]
                kept_all.append(sums[k, s][0])
                continue
            here, columns = slice(starts[k], starts[k] + spans[k]), slice(s * half, (s + 1) * half)
            residual = resid_in[here, columns].astype(F32) + total
            changed.append(residual.astype(BF16))
            slopes.append((scale[here] * (residual - target[here, columns])).astype(BF16))
            kept_all.append(slopes[-1])
        if changed:
            updated.append(jnp.concatenate(changed, axis=1))
            sloped.append(slopes)
        return kept_all

    for s in range(len(orders)):
        multiply(0, s, [])
    zero = 0.0
    for k in range(len(spans)):
        advance(k, 0.0)
        kept = advance(k, zero)
        if k + 1 == len(spans):
            break
        for s in range(len(orders)):
            kept = advance(k, multiply(k + 1, s, kept))
        while len(sloped) == k:
            kept = advance(k, 0.0)
        firsts.append(lax.all_gather(jnp.concatenate(sloped[k], axis=1), "dp"))
        zero = sum(nothing(b).astype(F32) for b in kept)
    while len(sloped) < len(spans):
        advance(len(spans) - 1, 0.0)

    gathered, streams = [], 4
    width = feats // streams
    for q in range(streams):
        s, at = divmod(q * width, half)
        block = gather_chips(sloped[-1][s][:, at : at + width], orders[q % 2][::-1])
        gathered.append((block, flip(block, "dp", 1)))
    return jnp.concatenate(updated), gradient(place, held, firsts, gathered)


def solution(mesh):
    in_specs = (
        P("dp", "shard"),
        P("shard", "dp"),
        P("dp", "shard"),
        P(("dp", "shard"), None),
        P("shard"),
        P(),
    )
    out_specs = (P("dp", "shard"), P("dp", "shard"))
    return jax.shard_map(
        per_device, mesh=mesh, in_specs=in_specs, out_specs=out_specs, check_vma=False
    )
```
